512 devices in a mesh: seq: 128 (over y, z, core), head: 4 (over x).
Axes of the slice: x: 4, y: 4, z: 16, core: 2. Of those that a mesh axis runs over, the one named last changes fastest.
Arguments:
- queries: bfloat16 [4, 4, 128, 32], P(None, 'head'), may hold values from -16 to 16
- keys: bfloat16 [4, 4, 128, 131072], P(None, 'head', None, 'seq'), may hold values from -48 to 48
- values: bfloat16 [4, 4, 128, 131072], P(None, 'head', None, 'seq'), may hold values from -6 to 6
- lengths: int32 [4], replicated, may hold values from 65536 to 131072, as said below
- offsets: int32 [4, 4], replicated, may hold values from 0 to 3, as said below
- out_proj: bfloat16 [4, 8, 128, 8192], P('head', None, None, 'seq'), may hold values from -0.23925781 to 0.23925781
Outputs:
- mixed: float32 [4, 4, 8192], P(None, None, 'seq')
The draws below stay inside these ranges and needn't reach their ends.
Inputs may be any that keep to these rules, and one draw needn't show every extreme that they name: `lengths`: every sequence holds at least 65536 positions; one sequence holds exactly 131072. `offsets`: each row is a permutation of 0 to 3.
All inputs are finite; a program needn't handle non-finite values.
Results may differ from the reference program's by a relative error of at most 0.0031.
Values sent between devices are 32-bit elements; how exact they have to be, the bound alone decides.
No kernel may reach another device: no remote copies, remote signals or barrier semaphores. Data moves between devices by JAX's collectives and lax.ppermute only.
A program may use at most 64 MiB of HBM per device.

```python
import jax
import jax.numpy as jnp

D = 8192
DH = 128
HEADS = 8
GROUPS = 4
DRAFT = 4
BATCH = 4
CTX_DEV = 1024
ROWS = 32
CTX = 131072
N_SEQ = 128


def draft_layout(key):
    base_lengths = jax.random.randint(jax.random.fold_in(key, 101), (BATCH,), CTX // 2, CTX + 1)
    full_index = jax.random.randint(jax.random.fold_in(key, 102), (), 0, BATCH)
    lengths = jnp.where(jnp.arange(BATCH) == full_index, CTX, base_lengths).astype(jnp.int32)
    row_keys = jax.random.split(jax.random.fold_in(key, 103), BATCH)
    offsets = jax.vmap(lambda row_key: jax.random.permutation(row_key, DRAFT))(row_keys).astype(jnp.int32)
    return (lengths, offsets)


def query_layout(key, align_weight):
    normal_part = 2.5 * jnp.clip(jax.random.normal(jax.random.fold_in(key, 107), (BATCH, GROUPS, DH, ROWS), jnp.float32), -4.0, 4.0)
    query_raw = normal_part
    direction = jnp.clip(jax.random.normal(jax.random.fold_in(key, 105), (BATCH, GROUPS, DH), jnp.float32), -3.0, 3.0)
    strength = 3.0 + jnp.minimum(jnp.arange(BATCH, dtype=jnp.float32), 2.0)
    aligned = (strength[:, None, None] * direction)[..., None]
    first_row = (jnp.arange(ROWS) == 0)[None, None, None, :] & (align_weight > 0.5)
    query_raw = jnp.where(first_row, aligned, query_raw)
    return query_raw


def draw_lengths(key, part):
    return draft_layout(key)[0]


def draw_offsets(key, part):
    return draft_layout(key)[1]


def draw_queries(key, part):
    query_raw = query_layout(key, 0.0)
    return query_raw.astype(jnp.bfloat16)


def draw_keys(key, part):
    lengths, offsets = draft_layout(key)
    query_raw = query_layout(key, 0.0)
    own_key = jax.random.fold_in(key, 7)
    positions = jnp.arange(CTX)
    key_field = jnp.clip(jax.random.normal(own_key, (BATCH, GROUPS, DH, CTX), jnp.float32), -4.0, 4.0)
    query_mean = jnp.mean(query_raw.reshape(BATCH, GROUPS, DH, DRAFT, HEADS), axis=-1)
    for draft_index in range(DRAFT):
        slot_pos = lengths - 1 - offsets[:, draft_index]
        slot_hit = positions[None, :] == slot_pos[:, None]
        key_field = key_field + jnp.where(slot_hit[:, None, None, :], query_mean[..., draft_index][..., None], 0.0)
    return key_field.astype(jnp.bfloat16)


def steps_of(stream_key, shape, shards, least, largest):
    gain = 1.0
    for position, blocks in shards:
        heights = jax.random.uniform(jax.random.fold_in(jax.random.fold_in(stream_key, 6), position), (blocks,), jnp.float32, least / len(shards), largest / len(shards))
        gain = gain * jnp.repeat(jnp.exp(heights), shape[position] // blocks).reshape((-1,) + (1,) * (len(shape) - 1 - position))
    return gain


def scatter_about(rng, shape, spread, limit, shards=(), kind=jnp.bfloat16):
    factor_of = steps_of(rng, shape, shards, -0.22, 0.18) if shards else 1.0
    drawn = jax.random.normal(rng, shape, jnp.float32) * spread * factor_of
    return jnp.minimum(jnp.maximum(drawn, -limit), limit).astype(kind)


def setup_inputs(seed: int = 0) -> dict:
    key_of = jax.random.split(jax.random.key(seed), 7)
    return {
        "queries": draw_queries(jax.random.fold_in(key_of[6], 71), 0),
        "keys": draw_keys(jax.random.fold_in(key_of[6], 71), 0),
        "values": scatter_about(key_of[2], (BATCH, GROUPS, DH, CTX), 1.0, 6.0, ((1, 4), (3, 128))),
        "lengths": draw_lengths(jax.random.fold_in(key_of[6], 71), 0),
        "offsets": draw_offsets(jax.random.fold_in(key_of[6], 71), 0),
        "out_proj": scatter_about(key_of[5], (GROUPS, HEADS, DH, D), 0.04, 0.23925781, ((0, 4), (3, 128))),
    }


masked_score = -1e30


def reference(queries, keys, values, lengths, offsets, out_proj):
    score_scale = DH ** -0.5
    positions = jnp.arange(CTX_DEV * N_SEQ, dtype=jnp.int32)
    results = []
    for seq_index in range(BATCH):
        scores = jnp.einsum("gdr,gdp->grp", queries[seq_index].astype(jnp.float32), keys[seq_index].astype(jnp.float32)) * score_scale
        visible = jnp.repeat(lengths[seq_index] - offsets[seq_index], HEADS)
        seen = positions[None, :] < visible[:, None]
        scores = jnp.where(seen[None], scores, masked_score).reshape(GROUPS, ROWS, N_SEQ, CTX_DEV)
        seen = seen.reshape(1, ROWS, N_SEQ, CTX_DEV)
        block_max = jnp.max(scores, axis=-1)
        weights = jnp.where(seen, jnp.exp(scores - block_max[..., None]), 0.0)
        block_sum = jnp.sum(weights, axis=-1)
        rounded = weights.astype(jnp.bfloat16)
        value_blocks = values[seq_index].reshape(GROUPS, DH, N_SEQ, CTX_DEV)
        block_out = jnp.einsum("grnp,gdnp->grnd", rounded.astype(jnp.float32), value_blocks.astype(jnp.float32))
        row_top = jnp.max(block_max, axis=-1)
        factor = jnp.exp(block_max - row_top[..., None])
        total = jnp.sum(block_sum * factor, axis=-1)
        summed = jnp.sum(block_out * factor[..., None], axis=2)
        attended = (summed / total[..., None]).astype(jnp.bfloat16)
        arranged = attended.reshape(GROUPS, DRAFT, HEADS, DH).transpose(1, 0, 2, 3).reshape(DRAFT, GROUPS * HEADS * DH)
        projected = jnp.dot(arranged, out_proj.reshape(GROUPS * HEADS * DH, D), preferred_element_type=jnp.float32)
        results.append(projected)
    return jnp.stack(results)
```

```python
import jax
import jax.numpy as jnp
from jax import lax
from jax.experimental import pallas as pl
from jax.experimental.pallas import tpu as pltpu
from jax.sharding import Mesh, PartitionSpec as P

masked_score = -1e30
Y, Z, CORES, HEAD = 4, 16, 2, 4
CHIPS = Y * Z
BATCH, DRAFT, HEADS, ROWS, DH, CTX_DEV, COLS = 4, 4, 8, 32, 128, 1024, 64
HALF = BATCH * ROWS // CORES
LANES = 128
vmem = pl.BlockSpec(memory_space=pltpu.VMEM)
smem = pl.BlockSpec(memory_space=pltpu.SMEM)
hbm = pl.BlockSpec(memory_space=pl.ANY)


def attend_block(lengths, offsets, queries, keys, values, out, held_keys, held_values, key_sems, value_sems):
    def key_copy(b):
        return pltpu.make_async_copy(keys.at[b, 0], held_keys.at[b], key_sems.at[b])

    def value_copy(b):
        return pltpu.make_async_copy(values.at[b, 0], held_values.at[b], value_sems.at[b])

    for b in range(BATCH):
        key_copy(b).start()
        value_copy(b).start()
    index = (lax.axis_index("y") * Z + lax.axis_index("z")) * CORES + lax.axis_index("core")
    positions = index * CTX_DEV + lax.broadcasted_iota(jnp.int32, (ROWS, CTX_DEV), 1)
    draft = lax.broadcasted_iota(jnp.int32, (ROWS, 1), 0) // HEADS
    lane = lax.broadcasted_iota(jnp.int32, (ROWS, LANES), 1)
    for b in range(BATCH):
        key_copy(b).wait()
        scores = lax.dot_general(
            queries[b, 0], held_keys[b], (((0,), (0,)), ((), ())), preferred_element_type=jnp.float32
        )
        scores = scores * DH ** (-0.5)
        offset = jnp.full((ROWS, 1), offsets[b, 0], jnp.int32)
        for j in range(1, DRAFT):
            offset = jnp.where(draft == j, offsets[b, j], offset)
        seen = positions < lengths[b] - offset
        scores = jnp.where(seen, scores, masked_score)
        block_max = jnp.max(scores, axis=1, keepdims=True)
        weights = jnp.where(seen, jnp.exp(scores - block_max), 0.0)
        block_sum = jnp.sum(weights, axis=1, keepdims=True)
        value_copy(b).wait()
        block_out = lax.dot_general(
            weights.astype(jnp.bfloat16),
            held_values[b],
            (((1,), (1,)), ((), ())),
            preferred_element_type=jnp.float32,
        )
        out[pl.ds(b * ROWS, ROWS), 0, :] = block_out
        out[pl.ds(b * ROWS, ROWS), 1, :] = jnp.where(lane < LANES // 2, block_max, block_sum)


def merge_pair(parts, out):
    lane = lax.broadcasted_iota(jnp.int32, (HALF, LANES), 1)
    stats = [parts[c, :, 1, :] for c in range(CORES)]
    tops = [s[:, :1] for s in stats]
    top = jnp.maximum(tops[0], tops[1])
    factors = [jnp.exp(t - top) for t in tops]
    total = sum(f * s[:, LANES // 2 : LANES // 2 + 1] for f, s in zip(factors, stats))
    out[:, 0, :] = sum(f * parts[c, :, 0, :] for c, f in enumerate(factors))
    out[:, 1, :] = jnp.where(lane < LANES // 2, top, total)


def merge_chips(parts, out):
    stats = parts[:, 1, :]
    tops = stats[:, :1]
    factor = jnp.exp(tops - jnp.max(tops, axis=0, keepdims=True))
    total = jnp.sum(factor * stats[:, LANES // 2 : LANES // 2 + 1], axis=0, keepdims=True)
    summed = jnp.sum(factor * parts[:, 0, :], axis=0, keepdims=True)
    out[...] = jnp.broadcast_to((summed / total)[None], out.shape)


def project(attended, out_proj, out):
    total = jnp.zeros((BATCH * DRAFT, COLS), jnp.float32)
    for h in range(HEADS):
        rows = attended[pl.ds(h, BATCH * DRAFT, stride=HEADS), :].astype(jnp.bfloat16)
        total += jnp.dot(rows, out_proj[0, h], preferred_element_type=jnp.float32)
    out[...] = total.reshape(BATCH, DRAFT, COLS)


def shards(queries, keys, values, lengths, offsets, out_proj):
    f32 = jnp.float32
    block = pl.pallas_call(
        attend_block,
        out_shape=jax.ShapeDtypeStruct((CORES * HALF, 2, LANES), f32),
        in_specs=[smem, smem, vmem, hbm, hbm],
        out_specs=vmem,
        scratch_shapes=[
            pltpu.VMEM((BATCH, DH, CTX_DEV), jnp.bfloat16),
            pltpu.VMEM((BATCH, DH, CTX_DEV), jnp.bfloat16),
            pltpu.SemaphoreType.DMA((BATCH,)),
            pltpu.SemaphoreType.DMA((BATCH,)),
        ],
        compiler_params=pltpu.CompilerParams(vmem_limit_bytes=16 * 2**20),
        name="attend_block",
    )(lengths, offsets, queries, keys, values)
    pair = lax.all_to_all(block.reshape(CORES, HALF, 2, LANES), "core", 0, 0, tiled=True)
    chip = pl.pallas_call(
        merge_pair,
        out_shape=jax.ShapeDtypeStruct((HALF, 2, LANES), f32),
        in_specs=[vmem],
        out_specs=vmem,
        name="merge_pair",
    )(pair)
    parts = lax.all_to_all(chip, ("y", "z"), 0, 0, tiled=True)
    copies = pl.pallas_call(
        merge_chips,
        out_shape=jax.ShapeDtypeStruct((CHIPS, 1, LANES), f32),
        in_specs=[vmem],
        out_specs=vmem,
        name="merge_chips",
    )(parts)
    rows = lax.all_to_all(copies, ("y", "z"), 0, 0, tiled=True)
    attended = lax.all_gather(rows, "core", axis=0, tiled=True).reshape(CORES * HALF, LANES)
    partial_out = pl.pallas_call(
        project,
        out_shape=jax.ShapeDtypeStruct((BATCH, DRAFT, COLS), f32),
        in_specs=[vmem, vmem],
        out_specs=vmem,
        name="project",
    )(attended, out_proj)
    return lax.psum(partial_out, "head")


def solution(mesh):
    fine = Mesh(mesh.devices.reshape(Y, Z, CORES, HEAD), ("y", "z", "core", "head"))
    seq = ("y", "z", "core")
    placed = (
        P(None, "head", None, None),
        P(None, "head", None, seq),
        P(None, "head", None, seq),
        P(),
        P(),
        P("head", None, None, seq),
    )
    return jax.shard_map(
        shards, mesh=fine, in_specs=placed, out_specs=P(None, None, seq), check_vma=False
    )
```

```python
import jax
import jax.numpy as jnp
from jax import lax
from jax.experimental import pallas as pl
from jax.experimental.pallas import tpu as pltpu
from jax.sharding import Mesh, PartitionSpec as P

masked_score = -1e30
Y, FAR, NEAR, CORES, HEAD = 4, 8, 2, 2, 4
BATCH, DRAFT, HEADS, ROWS, DH, CTX_DEV, COLS = 4, 4, 8, 32, 128, 1024, 64
TOKENS = BATCH * DRAFT
LANES = 128
near_axes = ("y", "near", "core")
vmem = pl.BlockSpec(memory_space=pltpu.VMEM)
smem = pl.BlockSpec(memory_space=pltpu.SMEM)
hbm = pl.BlockSpec(memory_space=pl.ANY)


def pack_stats(top, total):
    lane = lax.broadcasted_iota(jnp.int32, top.shape[:-1] + (LANES,), top.ndim - 1)
    return jnp.where(lane < LANES // 2, top, total)


def merge(parts):
    stats = parts[:, HEADS:, :]
    tops = stats[:, :, :1]
    top = jnp.max(tops, axis=0)
    factor = jnp.exp(tops - top[None])
    total = jnp.sum(factor * stats[:, :, LANES // 2 : LANES // 2 + 1], axis=0)
    summed = jnp.sum(factor * parts[:, :HEADS, :], axis=0)
    return top, total, summed


def attend_block(lengths, offsets, queries, keys, values, out, held_keys, held_values, key_sems, value_sems):
    def key_copy(b):
        return pltpu.make_async_copy(keys.at[b, 0], held_keys.at[b], key_sems.at[b])

    def value_copy(b):
        return pltpu.make_async_copy(values.at[b, 0], held_values.at[b], value_sems.at[b])

    for b in range(BATCH):
        key_copy(b).start()
        value_copy(b).start()
    chip = (lax.axis_index("y") * FAR + lax.axis_index("far")) * NEAR + lax.axis_index("near")
    index = chip * CORES + lax.axis_index("core")
    positions = index * CTX_DEV + lax.broadcasted_iota(jnp.int32, (ROWS, CTX_DEV), 1)
    draft = lax.broadcasted_iota(jnp.int32, (ROWS, 1), 0) // HEADS
    for b in range(BATCH):
        key_copy(b).wait()
        scores = jnp.dot(queries[b, 0], held_keys[b], preferred_element_type=jnp.float32)
        scores = scores * DH ** (-0.5)
        offset = jnp.full((ROWS, 1), offsets[b, 0], jnp.int32)
        for j in range(1, DRAFT):
            offset = jnp.where(draft == j, offsets[b, j], offset)
        seen = positions < lengths[b] - offset
        scores = jnp.where(seen, scores, masked_score)
        block_max = jnp.max(scores, axis=1, keepdims=True)
        weights = jnp.where(seen, jnp.exp(scores - block_max), 0.0)
        block_sum = jnp.sum(weights, axis=1, keepdims=True)
        value_copy(b).wait()
        block_out = lax.dot_general(
            weights.astype(jnp.bfloat16),
            held_values[b],
            (((1,), (1,)), ((), ())),
            preferred_element_type=jnp.float32,
        )
        tokens = pl.ds(b * DRAFT, DRAFT)
        out[tokens, :HEADS, :] = block_out.reshape(DRAFT, HEADS, LANES)
        out[tokens, HEADS:, :] = pack_stats(block_max, block_sum).reshape(DRAFT, HEADS, LANES)


def merge_near(parts, out):
    top, total, summed = merge(parts)
    out[:, :HEADS, :] = jnp.broadcast_to(summed[None], (FAR, HEADS, LANES))
    out[:, HEADS:, :] = jnp.broadcast_to(pack_stats(top, total)[None], (FAR, HEADS, LANES))


def merge_far(parts, out):
    _, total, summed = merge(parts)
    out[...] = jnp.broadcast_to((summed / total)[None], out.shape)


def project(attended, out_proj, out):
    total = jnp.zeros((TOKENS, COLS), jnp.float32)
    for h in range(HEADS):
        rows = attended[pl.ds(h, TOKENS, stride=HEADS), :].astype(jnp.bfloat16)
        total += lax.dot_general(
            rows, out_proj[0, h], (((1,), (1,)), ((), ())), preferred_element_type=jnp.float32
        )
    out[...] = total.reshape(BATCH, DRAFT, COLS)


def shards(queries, keys, values, lengths, offsets, out_proj):
    def packed(copies, rows):
        return jax.ShapeDtypeStruct((copies, rows, LANES), jnp.float32)

    block = pl.pallas_call(
        attend_block,
        out_shape=packed(TOKENS, 2 * HEADS),
        in_specs=[smem, smem, vmem, hbm, hbm],
        out_specs=vmem,
        scratch_shapes=[
            pltpu.VMEM((BATCH, DH, CTX_DEV), jnp.bfloat16),
            pltpu.VMEM((BATCH, DH, CTX_DEV), jnp.bfloat16),
            pltpu.SemaphoreType.DMA((BATCH,)),
            pltpu.SemaphoreType.DMA((BATCH,)),
        ],
        name="attend_block",
    )(lengths, offsets, queries.swapaxes(2, 3), keys, values)
    parts = lax.all_to_all(block, near_axes, 0, 0, tiled=True)
    copies = pl.pallas_call(
        merge_near, out_shape=packed(FAR, 2 * HEADS), in_specs=[vmem], out_specs=vmem, name="merge_near"
    )(parts)
    parts = lax.all_to_all(copies, "far", 0, 0, tiled=True)
    copies = pl.pallas_call(
        merge_far, out_shape=packed(TOKENS, HEADS), in_specs=[vmem], out_specs=vmem, name="merge_far"
    )(parts)
    rows = lax.all_to_all(copies, near_axes, 0, 0, tiled=True)
    partial_out = pl.pallas_call(
        project,
        out_shape=jax.ShapeDtypeStruct((BATCH, DRAFT, COLS), jnp.float32),
        in_specs=[vmem, vmem],
        out_specs=vmem,
        name="project",
    )(rows.reshape(TOKENS * HEADS, LANES), out_proj.swapaxes(2, 3))
    return lax.psum(partial_out, "head")


def solution(mesh):
    fine = Mesh(
        mesh.devices.reshape(Y, FAR, NEAR, CORES, HEAD), ("y", "far", "near", "core", "head")
    )
    seq = ("y", "far", "near", "core")
    placed = (
        P(None, "head", None, None),
        P(None, "head", None, seq),
        P(None, "head", None, seq),
        P(),
        P(),
        P("head", None, None, seq),
    )
    return jax.shard_map(
        shards, mesh=fine, in_specs=placed, out_specs=P(None, None, seq), check_vma=False
    )
```

```python
import jax
import jax.numpy as jnp
from jax import lax
from jax.experimental import pallas as pl
from jax.experimental.pallas import tpu as pltpu
from jax.sharding import Mesh, PartitionSpec as P

masked_score = -1e30
Y, FAR, NEAR, CORES, HEAD = 4, 8, 2, 2, 4
BATCH, DRAFT, HEADS, ROWS, DH, CTX_DEV, COLS = 4, 4, 8, 32, 128, 1024, 64
TOKENS = BATCH * DRAFT
LANES = 128
near_axes = ("y", "near", "core")
vmem = pl.BlockSpec(memory_space=pltpu.VMEM)
hbm = pl.BlockSpec(memory_space=pltpu.HBM)
attend_params = pltpu.CompilerParams(vmem_limit_bytes=8 * 2**20)
small_params = pltpu.CompilerParams(vmem_limit_bytes=2 * 2**20)


def in_hbm(x):
    return pltpu.with_memory_space_constraint(x, pltpu.HBM)


def pack_stats(top, total):
    lane = lax.broadcasted_iota(jnp.int32, top.shape[:-1] + (LANES,), top.ndim - 1)
    return jnp.where(lane < LANES // 2, top, total)


def merge(parts):
    stats = parts[:, HEADS:, :]
    tops = stats[:, :, :1]
    top = jnp.max(tops, axis=0)
    factor = jnp.exp(tops - top[None])
    total = jnp.sum(factor * stats[:, :, LANES // 2 : LANES // 2 + 1], axis=0)
    summed = jnp.sum(factor * parts[:, :HEADS, :], axis=0)
    return top, total, summed


def attend_block(lengths, offsets, queries, keys, values, out, *scratch):
    held_lengths, held_offsets, held_queries, held_keys, held_values, small_sems, key_sems, value_sems = scratch
    small = [
        pltpu.make_async_copy(source, target, small_sems.at[i])
        for i, (source, target) in enumerate(
            ((queries, held_queries), (lengths, held_lengths), (offsets, held_offsets))
        )
    ]
    key_copies = [
        pltpu.make_async_copy(keys.at[b, 0], held_keys.at[b], key_sems.at[b]) for b in range(BATCH)
    ]
    value_copies = [
        pltpu.make_async_copy(values.at[b, 0], held_values.at[b], value_sems.at[b])
        for b in range(BATCH)
    ]
    for copy in small + key_copies + value_copies:
        copy.start()
    chip = (lax.axis_index("y") * FAR + lax.axis_index("far")) * NEAR + lax.axis_index("near")
    index = chip * CORES + lax.axis_index("core")
    positions = index * CTX_DEV + lax.broadcasted_iota(jnp.int32, (ROWS, CTX_DEV), 1)
    draft = lax.broadcasted_iota(jnp.int32, (ROWS, 1), 0) // HEADS
    for copy in small:
        copy.wait()
    weights = []
    for b in range(BATCH):
        key_copies[b].wait()
        scores = jnp.dot(held_queries[b, 0], held_keys[b], preferred_element_type=jnp.float32)
        scores = scores * DH ** (-0.5)
        offset = jnp.full((ROWS, 1), held_offsets[b, 0], jnp.int32)
        for j in range(1, DRAFT):
            offset = jnp.where(draft == j, held_offsets[b, j], offset)
        seen = positions < held_lengths[b] - offset
        scores = jnp.where(seen, scores, masked_score)
        block_max = jnp.max(scores, axis=1, keepdims=True)
        weight = jnp.where(seen, jnp.exp(scores - block_max), 0.0)
        block_sum = jnp.sum(weight, axis=1, keepdims=True)
        weights.append(weight.astype(jnp.bfloat16))
        out[pl.ds(b * DRAFT, DRAFT), HEADS:, :] = pack_stats(block_max, block_sum).reshape(
            DRAFT, HEADS, LANES
        )
    for b in range(BATCH):
        value_copies[b].wait()
        block_out = lax.dot_general(
            weights[b], held_values[b], (((1,), (1,)), ((), ())), preferred_element_type=jnp.float32
        )
        out[pl.ds(b * DRAFT, DRAFT), :HEADS, :] = block_out.reshape(DRAFT, HEADS, LANES)


def merge_near(parts, out):
    top, total, summed = merge(parts)
    out[:, :HEADS, :] = jnp.broadcast_to(summed[None], (FAR, HEADS, LANES))
    out[:, HEADS:, :] = jnp.broadcast_to(pack_stats(top, total)[None], (FAR, HEADS, LANES))


def merge_far(parts, out):
    _, total, summed = merge(parts)
    out[...] = jnp.broadcast_to((summed / total)[None], out.shape)


def project(attended, out_proj, out):
    total = jnp.zeros((TOKENS, COLS), jnp.float32)
    for h in range(HEADS):
        rows = attended[pl.ds(h, TOKENS, stride=HEADS), :].astype(jnp.bfloat16)
        total += lax.dot_general(
            rows, out_proj[0, h], (((1,), (1,)), ((), ())), preferred_element_type=jnp.float32
        )
    out[...] = total.reshape(BATCH, DRAFT, COLS)


def shards(queries, keys, values, lengths, offsets, out_proj):
    def packed(copies, rows):
        return jax.ShapeDtypeStruct((copies, rows, LANES), jnp.float32)

    block = pl.pallas_call(
        attend_block,
        out_shape=packed(TOKENS, 2 * HEADS),
        in_specs=[hbm] * 5,
        out_specs=vmem,
        scratch_shapes=[
            pltpu.SMEM((BATCH,), jnp.int32),
            pltpu.SMEM((BATCH, DRAFT), jnp.int32),
            pltpu.VMEM((BATCH, 1, ROWS, DH), jnp.bfloat16),
            pltpu.VMEM((BATCH, DH, CTX_DEV), jnp.bfloat16),
            pltpu.VMEM((BATCH, DH, CTX_DEV), jnp.bfloat16),
            pltpu.SemaphoreType.DMA((3,)),
            pltpu.SemaphoreType.DMA((BATCH,)),
            pltpu.SemaphoreType.DMA((BATCH,)),
        ],
        compiler_params=attend_params,
        name="attend_block",
    )(*(in_hbm(x) for x in (lengths, offsets, queries.swapaxes(2, 3), keys, values)))
    parts = lax.all_to_all(block, near_axes, 0, 0, tiled=True)
    copies = pl.pallas_call(
        merge_near, out_shape=packed(FAR, 2 * HEADS), in_specs=[vmem], out_specs=vmem,
        compiler_params=small_params, name="merge_near"
    )(parts)
    parts = lax.all_to_all(copies, "far", 0, 0, tiled=True)
    copies = pl.pallas_call(
        merge_far, out_shape=packed(TOKENS, HEADS), in_specs=[vmem], out_specs=vmem,
        compiler_params=small_params, name="merge_far"
    )(parts)
    rows = lax.all_to_all(copies, near_axes, 0, 0, tiled=True)
    partial_out = pl.pallas_call(
        project,
        out_shape=jax.ShapeDtypeStruct((BATCH, DRAFT, COLS), jnp.float32),
        in_specs=[vmem, vmem],
        out_specs=vmem,
        compiler_params=small_params,
        name="project",
    )(rows.reshape(TOKENS * HEADS, LANES), out_proj.swapaxes(2, 3))
    return lax.psum(partial_out, "head")


def solution(mesh):
    fine = Mesh(
        mesh.devices.reshape(Y, FAR, NEAR, CORES, HEAD), ("y", "far", "near", "core", "head")
    )
    seq = ("y", "far", "near", "core")
    placed = (
        P(None, "head", None, None),
        P(None, "head", None, seq),
        P(None, "head", None, seq),
        P(),
        P(),
        P("head", None, None, seq),
    )
    return jax.shard_map(
        shards, mesh=fine, in_specs=placed, out_specs=P(None, None, seq), check_vma=False
    )
```

```python
import jax
import jax.numpy as jnp
from jax import lax
from jax.experimental import pallas as pl
from jax.experimental.pallas import tpu as pltpu
from jax.sharding import Mesh, PartitionSpec as P

masked_score = -1e30
Y, FAR, NEAR, CORES, HEAD = 4, 8, 2, 2, 4
BATCH, DRAFT, HEADS, ROWS, DH, CTX_DEV, COLS = 4, 4, 8, 32, 128, 1024, 64
TOKENS = BATCH * DRAFT
LANES = 128
near_order = [[11, 0, 1, 2, 3, 4, 5, 6, 7, 8, 9, 10, 12, 13, 14, 15]]
far_order = [[4, 5, 6, 7, 0, 1, 2, 3]]
head_order = [[2, 3, 0, 1]]
near_axes = ("y", "near", "core")
vmem = pl.BlockSpec(memory_space=pltpu.VMEM)
hbm = pl.BlockSpec(memory_space=pltpu.HBM)
attend_params = pltpu.CompilerParams(vmem_limit_bytes=8 * 2**20)
small_params = pltpu.CompilerParams(vmem_limit_bytes=2 * 2**20)


def in_hbm(x):
    return pltpu.with_memory_space_constraint(x, pltpu.HBM)


def pack_stats(top, total):
    lane = lax.broadcasted_iota(jnp.int32, top.shape[:-1] + (LANES,), top.ndim - 1)
    return jnp.where(lane < LANES // 2, top, total)


def merge(parts):
    stats = parts[:, HEADS:, :]
    tops = stats[:, :, :1]
    top = jnp.max(tops, axis=0)
    factor = jnp.exp(tops - top[None])
    total = jnp.sum(factor * stats[:, :, LANES // 2 : LANES // 2 + 1], axis=0)
    summed = jnp.sum(factor * parts[:, :HEADS, :], axis=0)
    return top, total, summed


def attend_block(lengths, offsets, queries, keys, values, out, *scratch):
    held_lengths, held_offsets, held_queries, held_keys, held_values, small_sems, key_sems, value_sems = scratch
    small = [
        pltpu.make_async_copy(source, target, small_sems.at[i])
        for i, (source, target) in enumerate(
            ((queries, held_queries), (lengths, held_lengths), (offsets, held_offsets))
        )
    ]
    key_copies = [
        pltpu.make_async_copy(keys.at[b, 0], held_keys.at[b], key_sems.at[b]) for b in range(BATCH)
    ]
    value_copies = [
        pltpu.make_async_copy(values.at[b, 0], held_values.at[b], value_sems.at[b])
        for b in range(BATCH)
    ]
    for copy in small + key_copies + value_copies:
        copy.start()
    chip = (lax.axis_index("y") * FAR + lax.axis_index("far")) * NEAR + lax.axis_index("near")
    index = chip * CORES + lax.axis_index("core")
    positions = index * CTX_DEV + lax.broadcasted_iota(jnp.int32, (ROWS, CTX_DEV), 1)
    draft = lax.broadcasted_iota(jnp.int32, (ROWS, 1), 0) // HEADS
    for copy in small:
        copy.wait()
    weights = []
    for b in range(BATCH):
        key_copies[b].wait()
        scores = jnp.dot(held_queries[b, 0], held_keys[b], preferred_element_type=jnp.float32)
        scores = scores * DH ** (-0.5)
        offset = jnp.full((ROWS, 1), held_offsets[b, 0], jnp.int32)
        for j in range(1, DRAFT):
            offset = jnp.where(draft == j, held_offsets[b, j], offset)
        seen = positions < held_lengths[b] - offset
        scores = jnp.where(seen, scores, masked_score)
        block_max = jnp.max(scores, axis=1, keepdims=True)
        weight = jnp.where(seen, jnp.exp(scores - block_max), 0.0)
        block_sum = jnp.sum(weight, axis=1, keepdims=True)
        weights.append(weight.astype(jnp.bfloat16))
        out[pl.ds(b * DRAFT, DRAFT), HEADS:, :] = pack_stats(block_max, block_sum).reshape(
            DRAFT, HEADS, LANES
        )
    for b in range(BATCH):
        value_copies[b].wait()
        block_out = lax.dot_general(
            weights[b], held_values[b], (((1,), (1,)), ((), ())), preferred_element_type=jnp.float32
        )
        out[pl.ds(b * DRAFT, DRAFT), :HEADS, :] = block_out.reshape(DRAFT, HEADS, LANES)


def merge_near(parts, out):
    top, total, summed = merge(parts)
    out[:, :HEADS, :] = jnp.broadcast_to(summed[None], (FAR, HEADS, LANES))
    out[:, HEADS:, :] = jnp.broadcast_to(pack_stats(top, total)[None], (FAR, HEADS, LANES))


def merge_far(parts, out):
    _, total, summed = merge(parts)
    out[...] = jnp.broadcast_to((summed / total)[None], out.shape)


def project(attended, out_proj, out):
    total = jnp.zeros((TOKENS, COLS), jnp.float32)
    for h in range(HEADS):
        rows = attended[pl.ds(h, TOKENS, stride=HEADS), :].astype(jnp.bfloat16)
        total += lax.dot_general(
            rows, out_proj[0, h], (((1,), (1,)), ((), ())), preferred_element_type=jnp.float32
        )
    packed = jnp.concatenate([total[: TOKENS // 2], total[TOKENS // 2 :]], axis=1)
    out[...] = jnp.broadcast_to(packed[None], out.shape)


def add_groups(terms, out):
    packed = jnp.sum(terms[...], axis=0)
    out[: BATCH // 2] = packed[:, :COLS].reshape(BATCH // 2, DRAFT, COLS)
    out[BATCH // 2 :] = packed[:, COLS:].reshape(BATCH // 2, DRAFT, COLS)


def shards(queries, keys, values, lengths, offsets, out_proj):
    def packed(copies, rows):
        return jax.ShapeDtypeStruct((copies, rows, LANES), jnp.float32)

    block = pl.pallas_call(
        attend_block,
        out_shape=packed(TOKENS, 2 * HEADS),
        in_specs=[hbm] * 5,
        out_specs=vmem,
        scratch_shapes=[
            pltpu.SMEM((BATCH,), jnp.int32),
            pltpu.SMEM((BATCH, DRAFT), jnp.int32),
            pltpu.VMEM((BATCH, 1, ROWS, DH), jnp.bfloat16),
            pltpu.VMEM((BATCH, DH, CTX_DEV), jnp.bfloat16),
            pltpu.VMEM((BATCH, DH, CTX_DEV), jnp.bfloat16),
            pltpu.SemaphoreType.DMA((3,)),
            pltpu.SemaphoreType.DMA((BATCH,)),
            pltpu.SemaphoreType.DMA((BATCH,)),
        ],
        compiler_params=attend_params,
        name="attend_block",
    )(*(in_hbm(x) for x in (lengths, offsets, queries.swapaxes(2, 3), keys, values)))
    parts = lax.all_to_all(block, near_axes, 0, 0, axis_index_groups=near_order, tiled=True)
    copies = pl.pallas_call(
        merge_near, out_shape=packed(FAR, 2 * HEADS), in_specs=[vmem], out_specs=vmem,
        compiler_params=small_params, name="merge_near"
    )(parts)
    parts = lax.all_to_all(copies, "far", 0, 0, axis_index_groups=far_order, tiled=True)
    copies = pl.pallas_call(
        merge_far, out_shape=packed(TOKENS, HEADS), in_specs=[vmem], out_specs=vmem,
        compiler_params=small_params, name="merge_far"
    )(parts)
    rows = lax.all_to_all(copies, near_axes, 0, 0, axis_index_groups=near_order, tiled=True)
    copies = pl.pallas_call(
        project,
        out_shape=packed(HEAD, TOKENS * COLS // LANES),
        in_specs=[vmem, vmem],
        out_specs=vmem,
        compiler_params=small_params,
        name="project",
    )(rows.reshape(TOKENS * HEADS, LANES), out_proj.swapaxes(2, 3))
    terms = lax.all_to_all(copies, "head", 0, 0, axis_index_groups=head_order, tiled=True)
    return pl.pallas_call(
        add_groups,
        out_shape=jax.ShapeDtypeStruct((BATCH, DRAFT, COLS), jnp.float32),
        in_specs=[vmem],
        out_specs=vmem,
        compiler_params=small_params,
        name="add_groups",
    )(terms)


def solution(mesh):
    fine = Mesh(
        mesh.devices.reshape(Y, FAR, NEAR, CORES, HEAD), ("y", "far", "near", "core", "head")
    )
    seq = ("y", "far", "near", "core")
    placed = (
        P(None, "head", None, None),
        P(None, "head", None, seq),
        P(None, "head", None, seq),
        P(),
        P(),
        P("head", None, None, seq),
    )
    return jax.shard_map(
        shards, mesh=fine, in_specs=placed, out_specs=P(None, None, seq), check_vma=False
    )
```

```python
import jax
import jax.numpy as jnp
from jax import lax
from jax.experimental import pallas as pl
from jax.experimental.pallas import tpu as pltpu
from jax.sharding import Mesh, PartitionSpec as P

masked_score = -1e30
Y, FAR, NEAR, CORES, HEAD = 4, 8, 2, 2, 4
BATCH, DRAFT, HEADS, ROWS, DH, CTX_DEV, COLS = 4, 4, 8, 32, 128, 1024, 64
TOKENS = BATCH * DRAFT
LANES = 128
SLOT = LANES // HEADS
MESSAGE = (HEADS + 1) * LANES
spread_order = [11, 0, 1, 2, 3, 4, 5, 6, 7, 8, 9, 10, 12, 13, 14, 15]
far_order = [9, 11, 13, 15, 1, 3, 5, 7, 8, 10, 12, 14, 0, 2, 4, 6]
far_halves = (1, 0)
gather_order = [5, 0, 1, 2, 3, 4, 6, 7]
head_order = [[2, 3, 0, 1]]
near_axes = ("y", "near", "core")
vmem = pl.BlockSpec(memory_space=pltpu.VMEM)
hbm = pl.BlockSpec(memory_space=pltpu.HBM)
attend_params = pltpu.CompilerParams(vmem_limit_bytes=8 * 2**20)
small_params = pltpu.CompilerParams(vmem_limit_bytes=2 * 2**20)


def in_hbm(x):
    return pltpu.with_memory_space_constraint(x, pltpu.HBM)


def stat_lanes(count):
    lane = lax.broadcasted_iota(jnp.int32, (count, LANES), 1)
    return lane // SLOT, lax.rem(lane, SLOT) < SLOT // 2


def merge(parts, some):
    stats = parts[some, 0, HEADS * LANES :]
    top = jnp.max(stats, axis=0, keepdims=True)
    factor = jnp.exp(stats - top)
    sums = pltpu.roll(stats, LANES - SLOT // 2, 1)
    total = jnp.sum(factor * sums, axis=0, keepdims=True)
    summed = []
    for h in range(HEADS):
        terms = factor[:, h * SLOT : h * SLOT + 1] * parts[some, 0, h * LANES : (h + 1) * LANES]
        summed.append(jnp.sum(terms, axis=0, keepdims=True))
    return top, total, summed


def attend_block(lengths, offsets, queries, keys, values, out, *scratch):
    held_lengths, held_offsets, held_queries, held_keys, held_values, small_sems, key_sems, value_sems = scratch
    small = [
        pltpu.make_async_copy(source, target, small_sems.at[i])
        for i, (source, target) in enumerate(
            ((queries, held_queries), (lengths, held_lengths), (offsets, held_offsets))
        )
    ]
    key_copies = [
        pltpu.make_async_copy(keys.at[b, 0], held_keys.at[b], key_sems.at[b]) for b in range(BATCH)
    ]
    value_copies = [
        pltpu.make_async_copy(values.at[b, 0], held_values.at[b], value_sems.at[b])
        for b in range(BATCH)
    ]
    for copy in small + key_copies + value_copies:
        copy.start()
    chip = (lax.axis_index("y") * FAR + lax.axis_index("far")) * NEAR + lax.axis_index("near")
    index = chip * CORES + lax.axis_index("core")
    positions = index * CTX_DEV + lax.broadcasted_iota(jnp.int32, (ROWS, CTX_DEV), 1)
    draft = lax.broadcasted_iota(jnp.int32, (ROWS, 1), 0) // HEADS
    head = lax.rem(lax.broadcasted_iota(jnp.int32, (ROWS, LANES), 0), HEADS)
    slot, is_top = stat_lanes(ROWS)
    for copy in small:
        copy.wait()
    for copy in key_copies:
        copy.wait()
    weights = []
    for b in range(BATCH):
        scores = jnp.dot(held_queries[b, 0], held_keys[b], preferred_element_type=jnp.float32)
        scores = scores * DH ** (-0.5)
        offset = jnp.full((ROWS, 1), held_offsets[b, 0], jnp.int32)
        for j in range(1, DRAFT):
            offset = jnp.where(draft == j, held_offsets[b, j], offset)
        seen = positions < held_lengths[b] - offset
        scores = jnp.where(seen, scores, masked_score)
        block_max = jnp.max(scores, axis=1, keepdims=True)
        weight = jnp.where(seen, jnp.exp(scores - block_max), 0.0)
        block_sum = jnp.sum(weight, axis=1, keepdims=True)
        weights.append(weight.astype(jnp.bfloat16))
        stats = jnp.where(is_top, block_max, block_sum)
        stats = jnp.where(head == slot, stats, 0.0).reshape(DRAFT, HEADS, LANES)
        stats = jnp.sum(stats, axis=1)
        for j in range(DRAFT):
            out[b * DRAFT + j, :, HEADS * LANES :] = stats[j : j + 1]
    for copy in value_copies:
        copy.wait()
    for b in range(BATCH):
        block_out = lax.dot_general(
            weights[b], held_values[b], (((1,), (1,)), ((), ())), preferred_element_type=jnp.float32
        )
        for j in range(DRAFT):
            for h in range(HEADS):
                row = block_out[j * HEADS + h : j * HEADS + h + 1]
                out[b * DRAFT + j, :, h * LANES : (h + 1) * LANES] = row


def merge_near(parts, out):
    top, total, summed = merge(parts, slice(0, TOKENS))
    _, is_top = stat_lanes(1)
    stats = jnp.where(is_top, top, pltpu.roll(total, SLOT // 2, 1))
    for h, row in enumerate(summed + [stats]):
        for i in range(FAR * NEAR):
            out[i, :, h * LANES : (h + 1) * LANES] = row


def merge_far(parts, out):
    for q in range(NEAR):
        _, total, summed = merge(parts, slice(q * FAR, (q + 1) * FAR))
        rows = [row / total[:, h * SLOT : h * SLOT + 1] for h, row in enumerate(summed)]
        rows = jnp.concatenate(rows, axis=0)
        out[:, q * HEADS : (q + 1) * HEADS, :] = jnp.broadcast_to(
            rows[None], (Y * CORES, HEADS, LANES)
        )


def project(attended, out_proj, out):
    total = jnp.zeros((TOKENS, COLS), jnp.float32)
    for h in range(HEADS):
        rows = attended[pl.ds(h, TOKENS, stride=HEADS), :].astype(jnp.bfloat16)
        total += lax.dot_general(
            rows, out_proj[0, h], (((1,), (1,)), ((), ())), preferred_element_type=jnp.float32
        )
    came = [(pair // CORES, q, pair % CORES) for pair in gather_order for q in far_halves]
    at = [came.index((d // (NEAR * CORES), d // CORES % NEAR, d % CORES)) for d in spread_order]
    rows = [total[i : i + 1] for i in at]
    packed = jnp.concatenate(
        [jnp.concatenate(half, axis=0) for half in (rows[: TOKENS // 2], rows[TOKENS // 2 :])], axis=1
    )
    out[...] = jnp.broadcast_to(packed[None], out.shape)


def add_groups(terms, out):
    packed = jnp.sum(terms[...], axis=0)
    out[: BATCH // 2] = packed[:, :COLS].reshape(BATCH // 2, DRAFT, COLS)
    out[BATCH // 2 :] = packed[:, COLS:].reshape(BATCH // 2, DRAFT, COLS)


def shards(queries, keys, values, lengths, offsets, out_proj):
    def packed(*shape):
        return jax.ShapeDtypeStruct(shape, jnp.float32)

    block = pl.pallas_call(
        attend_block,
        out_shape=packed(TOKENS, 1, MESSAGE),
        in_specs=[hbm] * 5,
        out_specs=vmem,
        scratch_shapes=[
            pltpu.SMEM((BATCH,), jnp.int32),
            pltpu.SMEM((BATCH, DRAFT), jnp.int32),
            pltpu.VMEM((BATCH, 1, ROWS, DH), jnp.bfloat16),
            pltpu.VMEM((BATCH, DH, CTX_DEV), jnp.bfloat16),
            pltpu.VMEM((BATCH, DH, CTX_DEV), jnp.bfloat16),
            pltpu.SemaphoreType.DMA((3,)),
            pltpu.SemaphoreType.DMA((BATCH,)),
            pltpu.SemaphoreType.DMA((BATCH,)),
        ],
        compiler_params=attend_params,
        name="attend_block",
    )(*(in_hbm(x) for x in (lengths, offsets, queries.swapaxes(2, 3), keys, values)))
    parts = lax.all_to_all(block, near_axes, 0, 0, axis_index_groups=[spread_order], tiled=True)
    copies = pl.pallas_call(
        merge_near, out_shape=packed(FAR * NEAR, 1, MESSAGE), in_specs=[vmem], out_specs=vmem,
        compiler_params=small_params, name="merge_near"
    )(parts)
    parts = lax.all_to_all(copies, ("far", "near"), 0, 0, axis_index_groups=[far_order], tiled=True)
    copies = pl.pallas_call(
        merge_far, out_shape=packed(Y * CORES, NEAR * HEADS, LANES), in_specs=[vmem], out_specs=vmem,
        compiler_params=small_params, name="merge_far"
    )(parts)
    rows = lax.all_to_all(copies, ("y", "core"), 0, 0, axis_index_groups=[gather_order], tiled=True)
    copies = pl.pallas_call(
        project,
        out_shape=packed(HEAD, TOKENS * COLS // LANES, LANES),
        in_specs=[vmem, vmem],
        out_specs=vmem,
        compiler_params=small_params,
        name="project",
    )(rows.reshape(TOKENS * HEADS, LANES), out_proj.swapaxes(2, 3))
    terms = lax.all_to_all(copies, "head", 0, 0, axis_index_groups=head_order, tiled=True)
    return pl.pallas_call(
        add_groups,
        out_shape=jax.ShapeDtypeStruct((BATCH, DRAFT, COLS), jnp.float32),
        in_specs=[vmem],
        out_specs=vmem,
        compiler_params=small_params,
        name="add_groups",
    )(terms)


def solution(mesh):
    fine = Mesh(
        mesh.devices.reshape(Y, FAR, NEAR, CORES, HEAD), ("y", "far", "near", "core", "head")
    )
    seq = ("y", "far", "near", "core")
    placed = (
        P(None, "head", None, None),
        P(None, "head", None, seq),
        P(None, "head", None, seq),
        P(),
        P(),
        P("head", None, None, seq),
    )
    return jax.shard_map(
        shards, mesh=fine, in_specs=placed, out_specs=P(None, None, seq), check_vma=False
    )
```

```python
import jax
import jax.numpy as jnp
from jax import lax
from jax.experimental import pallas as pl
from jax.experimental.pallas import tpu as pltpu
from jax.sharding import Mesh, PartitionSpec as P

masked_score = -1e30
left_out = -3e38
Y, FAR, NEAR, CORES, HEAD = 4, 8, 2, 2, 4
BATCH, DRAFT, HEADS, ROWS, DH, CTX_DEV, COLS = 4, 4, 8, 32, 128, 1024, 64
TOKENS = BATCH * DRAFT
LANES = 128
SLOT = LANES // HEADS
MESSAGE = (HEADS + 1) * LANES
spread_order = [11, 0, 1, 2, 3, 4, 5, 6, 7, 8, 9, 10, 12, 13, 14, 15]
far_order = [9, 8, 11, 10, 13, 12, 15, 14, 1, 0, 3, 2, 5, 4, 7, 6]
far_turns = (1, 0)
gather_order = [5, 0, 1, 2, 3, 4, 6, 7]
head_order = [[2, 3, 0, 1]]
near_axes = ("y", "near", "core")
vmem = pl.BlockSpec(memory_space=pltpu.VMEM)
hbm = pl.BlockSpec(memory_space=pltpu.HBM)
attend_params = pltpu.CompilerParams(vmem_limit_bytes=8 * 2**20)
small_params = pltpu.CompilerParams(vmem_limit_bytes=2 * 2**20)


def in_hbm(x):
    return pltpu.with_memory_space_constraint(x, pltpu.HBM)


def stat_lanes(count):
    lane = lax.broadcasted_iota(jnp.int32, (count, LANES), 1)
    return lane // SLOT, lax.rem(lane, SLOT) < SLOT // 2


def merge(parts, some=None):
    stats = parts[:, 0, HEADS * LANES :]
    counted = stats if some is None else jnp.where(some, stats, left_out)
    top = jnp.max(counted, axis=0, keepdims=True)
    factor = jnp.exp(counted - top)
    sums = pltpu.roll(stats, LANES - SLOT // 2, 1)
    total = jnp.sum(factor * sums, axis=0, keepdims=True)
    summed = []
    for h in range(HEADS):
        terms = factor[:, h * SLOT : h * SLOT + 1] * parts[:, 0, h * LANES : (h + 1) * LANES]
        summed.append(jnp.sum(terms, axis=0, keepdims=True))
    return top, total, summed


def attend_block(lengths, offsets, queries, keys, values, out, *scratch):
    held_lengths, held_offsets, held_queries, held_keys, held_values, small_sems, key_sem, value_sem = scratch
    small = [
        pltpu.make_async_copy(source, target, small_sems.at[i])
        for i, (source, target) in enumerate(
            ((queries, held_queries), (lengths, held_lengths), (offsets, held_offsets))
        )
    ]
    key_copy = pltpu.make_async_copy(keys, held_keys, key_sem)
    value_copy = pltpu.make_async_copy(values, held_values, value_sem)
    for copy in small + [key_copy, value_copy]:
        copy.start()
    chip = (lax.axis_index("y") * FAR + lax.axis_index("far")) * NEAR + lax.axis_index("near")
    index = chip * CORES + lax.axis_index("core")
    positions = index * CTX_DEV + lax.broadcasted_iota(jnp.int32, (ROWS, CTX_DEV), 1)
    draft = lax.broadcasted_iota(jnp.int32, (ROWS, 1), 0) // HEADS
    head = lax.rem(lax.broadcasted_iota(jnp.int32, (ROWS, LANES), 0), HEADS)
    slot, is_top = stat_lanes(ROWS)
    for copy in small:
        copy.wait()
    key_copy.wait()
    weights = []
    for b in range(BATCH):
        scores = jnp.dot(held_queries[b, 0], held_keys[b, 0], preferred_element_type=jnp.float32)
        scores = scores * DH ** (-0.5)
        offset = jnp.full((ROWS, 1), held_offsets[b, 0], jnp.int32)
        for j in range(1, DRAFT):
            offset = jnp.where(draft == j, held_offsets[b, j], offset)
        seen = positions < held_lengths[b] - offset
        scores = jnp.where(seen, scores, masked_score)
        block_max = jnp.max(scores, axis=1, keepdims=True)
        weight = jnp.where(seen, jnp.exp(scores - block_max), 0.0)
        block_sum = jnp.sum(weight, axis=1, keepdims=True)
        weights.append(weight.astype(jnp.bfloat16))
        stats = jnp.where(is_top, block_max, block_sum)
        stats = jnp.where(head == slot, stats, 0.0).reshape(DRAFT, HEADS, LANES)
        stats = jnp.sum(stats, axis=1)
        for j in range(DRAFT):
            out[b * DRAFT + j, :, HEADS * LANES :] = stats[j : j + 1]
    value_copy.wait()
    for b in range(BATCH):
        block_out = lax.dot_general(
            weights[b],
            held_values[b, 0], (((1,), (1,)), ((), ())), preferred_element_type=jnp.float32
        )
        for j in range(DRAFT):
            for h in range(HEADS):
                row = block_out[j * HEADS + h : j * HEADS + h + 1]
                out[b * DRAFT + j, :, h * LANES : (h + 1) * LANES] = row


def merge_near(parts, out):
    top, total, summed = merge(parts)
    _, is_top = stat_lanes(1)
    stats = jnp.where(is_top, top, pltpu.roll(total, SLOT // 2, 1))
    for h, row in enumerate(summed + [stats]):
        for i in range(FAR * NEAR):
            out[i, :, h * LANES : (h + 1) * LANES] = row


def merge_far(parts, out):
    source = lax.broadcasted_iota(jnp.int32, (FAR * NEAR, LANES), 0)
    for q in range(NEAR):
        _, total, summed = merge(parts, lax.rem(source, NEAR) == q)
        rows = [row / total[:, h * SLOT : h * SLOT + 1] for h, row in enumerate(summed)]
        rows = jnp.concatenate(rows, axis=0)
        out[:, q * HEADS : (q + 1) * HEADS, :] = jnp.broadcast_to(
            rows[None], (Y * CORES, HEADS, LANES)
        )


def project(attended, out_proj, out):
    total = jnp.zeros((TOKENS, COLS), jnp.float32)
    for h in range(HEADS):
        rows = attended[pl.ds(h, TOKENS, stride=HEADS), :].astype(jnp.bfloat16)
        total += lax.dot_general(
            rows, out_proj[0, h], (((1,), (1,)), ((), ())), preferred_element_type=jnp.float32
        )
    came = [(pair // CORES, q, pair % CORES) for pair in gather_order for q in far_turns]
    at = [came.index((d // (NEAR * CORES), d // CORES % NEAR, d % CORES)) for d in spread_order]
    rows = [total[i : i + 1] for i in at]
    packed = jnp.concatenate(
        [jnp.concatenate(half, axis=0) for half in (rows[: TOKENS // 2], rows[TOKENS // 2 :])], axis=1
    )
    out[...] = jnp.broadcast_to(packed[None], out.shape)


def add_groups(terms, out):
    packed = jnp.sum(terms[...], axis=0)
    out[: BATCH // 2] = packed[:, :COLS].reshape(BATCH // 2, DRAFT, COLS)
    out[BATCH // 2 :] = packed[:, COLS:].reshape(BATCH // 2, DRAFT, COLS)


def shards(queries, keys, values, lengths, offsets, out_proj):
    def packed(*shape):
        return jax.ShapeDtypeStruct(shape, jnp.float32)

    block = pl.pallas_call(
        attend_block,
        out_shape=packed(TOKENS, 1, MESSAGE),
        in_specs=[hbm] * 5,
        out_specs=vmem,
        scratch_shapes=[
            pltpu.SMEM((BATCH,), jnp.int32),
            pltpu.SMEM((BATCH, DRAFT), jnp.int32),
            pltpu.VMEM((BATCH, 1, ROWS, DH), jnp.bfloat16),
            pltpu.VMEM((BATCH, 1, DH, CTX_DEV), jnp.bfloat16),
            pltpu.VMEM((BATCH, 1, DH, CTX_DEV), jnp.bfloat16),
            pltpu.SemaphoreType.DMA((3,)),
            pltpu.SemaphoreType.DMA,
            pltpu.SemaphoreType.DMA,
        ],
        compiler_params=attend_params,
        name="attend_block",
    )(*(in_hbm(x) for x in (lengths, offsets, queries.swapaxes(2, 3), keys, values)))
    parts = lax.all_to_all(block, near_axes, 0, 0, axis_index_groups=[spread_order], tiled=True)
    copies = pl.pallas_call(
        merge_near, out_shape=packed(FAR * NEAR, 1, MESSAGE), in_specs=[vmem], out_specs=vmem,
        compiler_params=small_params, name="merge_near"
    )(parts)
    parts = lax.all_to_all(copies, ("far", "near"), 0, 0, axis_index_groups=[far_order], tiled=True)
    copies = pl.pallas_call(
        merge_far, out_shape=packed(Y * CORES, NEAR * HEADS, LANES), in_specs=[vmem], out_specs=vmem,
        compiler_params=small_params, name="merge_far"
    )(parts)
    rows = lax.all_to_all(copies, ("y", "core"), 0, 0, axis_index_groups=[gather_order], tiled=True)
    copies = pl.pallas_call(
        project,
        out_shape=packed(HEAD, TOKENS * COLS // LANES, LANES),
        in_specs=[vmem, vmem],
        out_specs=vmem,
        compiler_params=small_params,
        name="project",
    )(rows.reshape(TOKENS * HEADS, LANES), out_proj.swapaxes(2, 3))
    terms = lax.all_to_all(copies, "head", 0, 0, axis_index_groups=head_order, tiled=True)
    return pl.pallas_call(
        add_groups,
        out_shape=jax.ShapeDtypeStruct((BATCH, DRAFT, COLS), jnp.float32),
        in_specs=[vmem],
        out_specs=vmem,
        compiler_params=small_params,
        name="add_groups",
    )(terms)


def solution(mesh):
    fine = Mesh(
        mesh.devices.reshape(Y, FAR, NEAR, CORES, HEAD), ("y", "far", "near", "core", "head")
    )
    seq = ("y", "far", "near", "core")
    placed = (
        P(None, "head", None, None),
        P(None, "head", None, seq),
        P(None, "head", None, seq),
        P(),
        P(),
        P("head", None, None, seq),
    )
    return jax.shard_map(
        shards, mesh=fine, in_specs=placed, out_specs=P(None, None, seq), check_vma=False
    )
```

```python
import jax
import jax.numpy as jnp
from jax import lax
from jax.experimental import pallas as pl
from jax.experimental.pallas import tpu as pltpu
from jax.sharding import Mesh, PartitionSpec as P

masked_score = -1e30
Y, FAR, NEAR, CORES, HEAD = 4, 8, 2, 2, 4
BATCH, DRAFT, HEADS, ROWS, DH, CTX_DEV, COLS = 4, 4, 8, 32, 128, 1024, 64
TOKENS = BATCH * DRAFT
LANES = 128
SLOT = LANES // HEADS
MESSAGE = (HEADS + 1) * LANES
near_order = [[11, 0, 1, 2, 3, 4, 5, 6, 7, 8, 9, 10, 12, 13, 14, 15]]
far_order = [[5, 6, 7, 0, 1, 2, 3, 4]]
head_order = [[2, 3, 0, 1]]
near_axes = ("y", "near", "core")
vmem = pl.BlockSpec(memory_space=pltpu.VMEM)
hbm = pl.BlockSpec(memory_space=pltpu.HBM)
attend_params = pltpu.CompilerParams(vmem_limit_bytes=8 * 2**20)
small_params = pltpu.CompilerParams(vmem_limit_bytes=2 * 2**20)


def in_hbm(x):
    return pltpu.with_memory_space_constraint(x, pltpu.HBM)


def stat_lanes(count):
    lane = lax.broadcasted_iota(jnp.int32, (count, LANES), 1)
    return lane // SLOT, lax.rem(lane, SLOT) < SLOT // 2


def merge(parts):
    stats = parts[:, 0, HEADS * LANES :]
    top = jnp.max(stats, axis=0, keepdims=True)
    factor = jnp.exp(stats - top)
    sums = pltpu.roll(stats, LANES - SLOT // 2, 1)
    total = jnp.sum(factor * sums, axis=0, keepdims=True)
    summed = []
    for h in range(HEADS):
        terms = factor[:, h * SLOT : h * SLOT + 1] * parts[:, 0, h * LANES : (h + 1) * LANES]
        summed.append(jnp.sum(terms, axis=0, keepdims=True))
    return top, total, summed


def attend_block(lengths, offsets, queries, keys, values, out, *scratch):
    held_lengths, held_offsets, held_queries, held_keys, held_values, small_sems, key_sem, value_sem = scratch
    small = [
        pltpu.make_async_copy(source, target, small_sems.at[i])
        for i, (source, target) in enumerate(
            ((queries, held_queries), (lengths, held_lengths), (offsets, held_offsets))
        )
    ]
    key_copy = pltpu.make_async_copy(keys, held_keys, key_sem)
    value_copy = pltpu.make_async_copy(values, held_values, value_sem)
    for copy in small + [key_copy, value_copy]:
        copy.start()
    chip = (lax.axis_index("y") * FAR + lax.axis_index("far")) * NEAR + lax.axis_index("near")
    index = chip * CORES + lax.axis_index("core")
    positions = index * CTX_DEV + lax.broadcasted_iota(jnp.int32, (ROWS, CTX_DEV), 1)
    draft = lax.broadcasted_iota(jnp.int32, (ROWS, 1), 0) // HEADS
    head = lax.rem(lax.broadcasted_iota(jnp.int32, (ROWS, LANES), 0), HEADS)
    slot, is_top = stat_lanes(ROWS)
    for copy in small:
        copy.wait()
    key_copy.wait()
    weights = []
    for b in range(BATCH):
        scores = jnp.dot(held_queries[b, 0], held_keys[b, 0], preferred_element_type=jnp.float32)
        scores = scores * DH ** (-0.5)
        offset = jnp.full((ROWS, 1), held_offsets[b, 0], jnp.int32)
        for j in range(1, DRAFT):
            offset = jnp.where(draft == j, held_offsets[b, j], offset)
        seen = positions < held_lengths[b] - offset
        scores = jnp.where(seen, scores, masked_score)
        block_max = jnp.max(scores, axis=1, keepdims=True)
        weight = jnp.where(seen, jnp.exp(scores - block_max), 0.0)
        block_sum = jnp.sum(weight, axis=1, keepdims=True)
        weights.append(weight.astype(jnp.bfloat16))
        stats = jnp.where(is_top, block_max, block_sum)
        stats = jnp.where(head == slot, stats, 0.0).reshape(DRAFT, HEADS, LANES)
        stats = jnp.sum(stats, axis=1)
        for j in range(DRAFT):
            out[b * DRAFT + j, :, HEADS * LANES :] = stats[j : j + 1]
    value_copy.wait()
    for b in range(BATCH):
        block_out = lax.dot_general(
            weights[b],
            held_values[b, 0], (((1,), (1,)), ((), ())), preferred_element_type=jnp.float32
        )
        for j in range(DRAFT):
            for h in range(HEADS):
                row = block_out[j * HEADS + h : j * HEADS + h + 1]
                out[b * DRAFT + j, :, h * LANES : (h + 1) * LANES] = row


def merge_near(parts, out):
    top, total, summed = merge(parts)
    _, is_top = stat_lanes(1)
    stats = jnp.where(is_top, top, pltpu.roll(total, SLOT // 2, 1))
    for h, row in enumerate(summed + [stats]):
        for i in range(FAR):
            out[i, :, h * LANES : (h + 1) * LANES] = row


def merge_far(parts, out):
    _, total, summed = merge(parts)
    rows = [row / total[:, h * SLOT : h * SLOT + 1] for h, row in enumerate(summed)]
    out[...] = jnp.broadcast_to(jnp.concatenate(rows, axis=0)[None], out.shape)


def project(attended, out_proj, out):
    total = jnp.zeros((TOKENS, COLS), jnp.float32)
    for h in range(HEADS):
        rows = attended[pl.ds(h, TOKENS, stride=HEADS), :].astype(jnp.bfloat16)
        total += lax.dot_general(
            rows, out_proj[0, h], (((1,), (1,)), ((), ())), preferred_element_type=jnp.float32
        )
    packed = jnp.concatenate([total[: TOKENS // 2], total[TOKENS // 2 :]], axis=1)
    out[...] = jnp.broadcast_to(packed[None], out.shape)


def add_groups(terms, out):
    packed = jnp.sum(terms[...], axis=0)
    out[: BATCH // 2] = packed[:, :COLS].reshape(BATCH // 2, DRAFT, COLS)
    out[BATCH // 2 :] = packed[:, COLS:].reshape(BATCH // 2, DRAFT, COLS)


def shards(queries, keys, values, lengths, offsets, out_proj):
    def packed(*shape):
        return jax.ShapeDtypeStruct(shape, jnp.float32)

    block = pl.pallas_call(
        attend_block,
        out_shape=packed(TOKENS, 1, MESSAGE),
        in_specs=[hbm] * 5,
        out_specs=vmem,
        scratch_shapes=[
            pltpu.SMEM((BATCH,), jnp.int32),
            pltpu.SMEM((BATCH, DRAFT), jnp.int32),
            pltpu.VMEM((BATCH, 1, ROWS, DH), jnp.bfloat16),
            pltpu.VMEM((BATCH, 1, DH, CTX_DEV), jnp.bfloat16),
            pltpu.VMEM((BATCH, 1, DH, CTX_DEV), jnp.bfloat16),
            pltpu.SemaphoreType.DMA((3,)),
            pltpu.SemaphoreType.DMA,
            pltpu.SemaphoreType.DMA,
        ],
        compiler_params=attend_params,
        name="attend_block",
    )(*(in_hbm(x) for x in (lengths, offsets, queries.swapaxes(2, 3), keys, values)))
    parts = lax.all_to_all(block, near_axes, 0, 0, axis_index_groups=near_order, tiled=True)
    copies = pl.pallas_call(
        merge_near, out_shape=packed(FAR, 1, MESSAGE), in_specs=[vmem], out_specs=vmem,
        compiler_params=small_params, name="merge_near"
    )(parts)
    parts = lax.all_to_all(copies, "far", 0, 0, axis_index_groups=far_order, tiled=True)
    copies = pl.pallas_call(
        merge_far, out_shape=packed(TOKENS, HEADS, LANES), in_specs=[vmem], out_specs=vmem,
        compiler_params=small_params, name="merge_far"
    )(parts)
    rows = lax.all_to_all(copies, near_axes, 0, 0, axis_index_groups=near_order, tiled=True)
    copies = pl.pallas_call(
        project,
        out_shape=packed(HEAD, TOKENS * COLS // LANES, LANES),
        in_specs=[vmem, vmem],
        out_specs=vmem,
        compiler_params=small_params,
        name="project",
    )(rows.reshape(TOKENS * HEADS, LANES), out_proj.swapaxes(2, 3))
    terms = lax.all_to_all(copies, "head", 0, 0, axis_index_groups=head_order, tiled=True)
    return pl.pallas_call(
        add_groups,
        out_shape=jax.ShapeDtypeStruct((BATCH, DRAFT, COLS), jnp.float32),
        in_specs=[vmem],
        out_specs=vmem,
        compiler_params=small_params,
        name="add_groups",
    )(terms)


def solution(mesh):
    fine = Mesh(
        mesh.devices.reshape(Y, FAR, NEAR, CORES, HEAD), ("y", "far", "near", "core", "head")
    )
    seq = ("y", "far", "near", "core")
    placed = (
        P(None, "head", None, None),
        P(None, "head", None, seq),
        P(None, "head", None, seq),
        P(),
        P(),
        P("head", None, None, seq),
    )
    return jax.shard_map(
        shards, mesh=fine, in_specs=placed, out_specs=P(None, None, seq), check_vma=False
    )
```

```python
import jax
import jax.numpy as jnp
from jax import lax
from jax.experimental import pallas as pl
from jax.experimental.pallas import tpu as pltpu
from jax.sharding import Mesh, PartitionSpec as P

masked_score = -1e30
Y, FAR, NEAR, CORES, HEAD = 4, 8, 2, 2, 4
BATCH, DRAFT, HEADS, ROWS, DH, CTX_DEV, COLS = 4, 4, 8, 32, 128, 1024, 64
TOKENS = BATCH * DRAFT
LANES = 128
SLOT = LANES // HEADS
MESSAGE = (HEADS + 1) * LANES
near_order = [[11, 0, 1, 2, 3, 4, 5, 6, 7, 8, 9, 10, 12, 13, 14, 15]]
far_order = [[10, 12, 14, 0, 2, 4, 6, 8], [9, 11, 13, 15, 1, 3, 5, 7]]
head_order = [[2, 3, 0, 1]]
near_axes = ("y", "near", "core")
vmem = pl.BlockSpec(memory_space=pltpu.VMEM)
hbm = pl.BlockSpec(memory_space=pltpu.HBM)
attend_params = pltpu.CompilerParams(vmem_limit_bytes=8 * 2**20)
small_params = pltpu.CompilerParams(vmem_limit_bytes=2 * 2**20)


def in_hbm(x):
    return pltpu.with_memory_space_constraint(x, pltpu.HBM)


def stat_lanes(count):
    lane = lax.broadcasted_iota(jnp.int32, (count, LANES), 1)
    return lane // SLOT, lax.rem(lane, SLOT) < SLOT // 2


def merge(parts):
    stats = parts[:, 0, HEADS * LANES :]
    top = jnp.max(stats, axis=0, keepdims=True)
    factor = jnp.exp(stats - top)
    sums = pltpu.roll(stats, LANES - SLOT // 2, 1)
    total = jnp.sum(factor * sums, axis=0, keepdims=True)
    summed = []
    for h in range(HEADS):
        terms = factor[:, h * SLOT : h * SLOT + 1] * parts[:, 0, h * LANES : (h + 1) * LANES]
        summed.append(jnp.sum(terms, axis=0, keepdims=True))
    return top, total, summed


def attend_block(lengths, offsets, queries, keys, values, out, *scratch):
    held_lengths, held_offsets, held_queries, held_keys, held_values, small_sems, key_sem, value_sem = scratch
    small = [
        pltpu.make_async_copy(source, target, small_sems.at[i])
        for i, (source, target) in enumerate(
            ((queries, held_queries), (lengths, held_lengths), (offsets, held_offsets))
        )
    ]
    key_copy = pltpu.make_async_copy(keys, held_keys, key_sem)
    value_copy = pltpu.make_async_copy(values, held_values, value_sem)
    for copy in small + [key_copy, value_copy]:
        copy.start()
    chip = (lax.axis_index("y") * FAR + lax.axis_index("far")) * NEAR + lax.axis_index("near")
    index = chip * CORES + lax.axis_index("core")
    positions = index * CTX_DEV + lax.broadcasted_iota(jnp.int32, (ROWS, CTX_DEV), 1)
    draft = lax.broadcasted_iota(jnp.int32, (ROWS, 1), 0) // HEADS
    head = lax.rem(lax.broadcasted_iota(jnp.int32, (ROWS, LANES), 0), HEADS)
    slot, is_top = stat_lanes(ROWS)
    for copy in small:
        copy.wait()
    key_copy.wait()
    weights = []
    for b in range(BATCH):
        scores = jnp.dot(held_queries[b, 0], held_keys[b, 0], preferred_element_type=jnp.float32)
        scores = scores * DH ** (-0.5)
        offset = jnp.full((ROWS, 1), held_offsets[b, 0], jnp.int32)
        for j in range(1, DRAFT):
            offset = jnp.where(draft == j, held_offsets[b, j], offset)
        seen = positions < held_lengths[b] - offset
        scores = jnp.where(seen, scores, masked_score)
        block_max = jnp.max(scores, axis=1, keepdims=True)
        weight = jnp.where(seen, jnp.exp(scores - block_max), 0.0)
        block_sum = jnp.sum(weight, axis=1, keepdims=True)
        weights.append(weight.astype(jnp.bfloat16))
        stats = jnp.where(is_top, block_max, block_sum)
        stats = jnp.where(head == slot, stats, 0.0).reshape(DRAFT, HEADS, LANES)
        stats = jnp.sum(stats, axis=1)
        for j in range(DRAFT):
            out[b * DRAFT + j, :, HEADS * LANES :] = stats[j : j + 1]
    value_copy.wait()
    for b in range(BATCH):
        block_out = lax.dot_general(
            weights[b],
            held_values[b, 0], (((1,), (1,)), ((), ())), preferred_element_type=jnp.float32
        )
        for j in range(DRAFT):
            for h in range(HEADS):
                row = block_out[j * HEADS + h : j * HEADS + h + 1]
                out[b * DRAFT + j, :, h * LANES : (h + 1) * LANES] = row


def merge_near(parts, out):
    top, total, summed = merge(parts)
    _, is_top = stat_lanes(1)
    stats = jnp.where(is_top, top, pltpu.roll(total, SLOT // 2, 1))
    for h, row in enumerate(summed + [stats]):
        for i in range(FAR):
            out[i, :, h * LANES : (h + 1) * LANES] = row


def merge_far(parts, out):
    _, total, summed = merge(parts)
    rows = [row / total[:, h * SLOT : h * SLOT + 1] for h, row in enumerate(summed)]
    out[...] = jnp.broadcast_to(jnp.concatenate(rows, axis=0)[None], out.shape)


def project(attended, out_proj, out):
    total = jnp.zeros((TOKENS, COLS), jnp.float32)
    for h in range(HEADS):
        rows = attended[pl.ds(h, TOKENS, stride=HEADS), :].astype(jnp.bfloat16)
        total += lax.dot_general(
            rows, out_proj[0, h], (((1,), (1,)), ((), ())), preferred_element_type=jnp.float32
        )
    packed = jnp.concatenate([total[: TOKENS // 2], total[TOKENS // 2 :]], axis=1)
    out[...] = jnp.broadcast_to(packed[None], out.shape)


def add_groups(terms, out):
    packed = jnp.sum(terms[...], axis=0)
    out[: BATCH // 2] = packed[:, :COLS].reshape(BATCH // 2, DRAFT, COLS)
    out[BATCH // 2 :] = packed[:, COLS:].reshape(BATCH // 2, DRAFT, COLS)


def shards(queries, keys, values, lengths, offsets, out_proj):
    def packed(*shape):
        return jax.ShapeDtypeStruct(shape, jnp.float32)

    block = pl.pallas_call(
        attend_block,
        out_shape=packed(TOKENS, 1, MESSAGE),
        in_specs=[hbm] * 5,
        out_specs=vmem,
        scratch_shapes=[
            pltpu.SMEM((BATCH,), jnp.int32),
            pltpu.SMEM((BATCH, DRAFT), jnp.int32),
            pltpu.VMEM((BATCH, 1, ROWS, DH), jnp.bfloat16),
            pltpu.VMEM((BATCH, 1, DH, CTX_DEV), jnp.bfloat16),
            pltpu.VMEM((BATCH, 1, DH, CTX_DEV), jnp.bfloat16),
            pltpu.SemaphoreType.DMA((3,)),
            pltpu.SemaphoreType.DMA,
            pltpu.SemaphoreType.DMA,
        ],
        compiler_params=attend_params,
        name="attend_block",
    )(*(in_hbm(x) for x in (lengths, offsets, queries.swapaxes(2, 3), keys, values)))
    parts = lax.all_to_all(block, near_axes, 0, 0, axis_index_groups=near_order, tiled=True)
    copies = pl.pallas_call(
        merge_near, out_shape=packed(FAR, 1, MESSAGE), in_specs=[vmem], out_specs=vmem,
        compiler_params=small_params, name="merge_near"
    )(parts)
    parts = lax.all_to_all(
        copies, ("far", "near"), 0, 0, axis_index_groups=far_order, tiled=True
    )
    copies = pl.pallas_call(
        merge_far, out_shape=packed(TOKENS, HEADS, LANES), in_specs=[vmem], out_specs=vmem,
        compiler_params=small_params, name="merge_far"
    )(parts)
    rows = lax.all_to_all(copies, near_axes, 0, 0, axis_index_groups=near_order, tiled=True)
    copies = pl.pallas_call(
        project,
        out_shape=packed(HEAD, TOKENS * COLS // LANES, LANES),
        in_specs=[vmem, vmem],
        out_specs=vmem,
        compiler_params=small_params,
        name="project",
    )(rows.reshape(TOKENS * HEADS, LANES), out_proj.swapaxes(2, 3))
    terms = lax.all_to_all(copies, "head", 0, 0, axis_index_groups=head_order, tiled=True)
    return pl.pallas_call(
        add_groups,
        out_shape=jax.ShapeDtypeStruct((BATCH, DRAFT, COLS), jnp.float32),
        in_specs=[vmem],
        out_specs=vmem,
        compiler_params=small_params,
        name="add_groups",
    )(terms)


def solution(mesh):
    fine = Mesh(
        mesh.devices.reshape(Y, FAR, NEAR, CORES, HEAD), ("y", "far", "near", "core", "head")
    )
    seq = ("y", "far", "near", "core")
    placed = (
        P(None, "head", None, None),
        P(None, "head", None, seq),
        P(None, "head", None, seq),
        P(),
        P(),
        P("head", None, None, seq),
    )
    return jax.shard_map(
        shards, mesh=fine, in_specs=placed, out_specs=P(None, None, seq), check_vma=False
    )
```

```python
import jax
import jax.numpy as jnp
from jax import lax
from jax.experimental import pallas as pl
from jax.experimental.pallas import tpu as pltpu
from jax.sharding import Mesh, PartitionSpec as P

masked_score = -1e30
Y, FAR, NEAR, CORES, HEAD = 4, 8, 2, 2, 4
BATCH, DRAFT, HEADS, ROWS, DH, CTX_DEV, COLS = 4, 4, 8, 32, 128, 1024, 64
TOKENS = BATCH * DRAFT
LANES = 128
SLOT = LANES // HEADS
MESSAGE = (HEADS + 1) * LANES
near_order = [[11, 0, 1, 2, 3, 4, 5, 6, 7, 8, 9, 10, 12, 13, 14, 15]]
far_order = [[10, 12, 14, 0, 2, 4, 6, 8], [9, 11, 13, 15, 1, 3, 5, 7]]
head_order = [[2, 3, 0, 1]]
near_axes = ("y", "near", "core")
vmem = pl.BlockSpec(memory_space=pltpu.VMEM)
hbm = pl.BlockSpec(memory_space=pltpu.HBM)
attend_params = pltpu.CompilerParams(vmem_limit_bytes=8 * 2**20)
small_params = pltpu.CompilerParams(vmem_limit_bytes=2 * 2**20)


def in_hbm(x):
    return pltpu.with_memory_space_constraint(x, pltpu.HBM)


def stat_lanes(count):
    lane = lax.broadcasted_iota(jnp.int32, (count, LANES), 1)
    return lane // SLOT, lax.rem(lane, SLOT) < SLOT // 2


def merge(parts):
    stats = parts[:, 0, HEADS * LANES :]
    top = jnp.max(stats, axis=0, keepdims=True)
    factor = jnp.exp(stats - top)
    sums = pltpu.roll(stats, LANES - SLOT // 2, 1)
    total = jnp.sum(factor * sums, axis=0, keepdims=True)
    summed = []
    for h in range(HEADS):
        terms = factor[:, h * SLOT : h * SLOT + 1] * parts[:, 0, h * LANES : (h + 1) * LANES]
        summed.append(jnp.sum(terms, axis=0, keepdims=True))
    return top, total, summed


def attend_block(lengths, offsets, queries, keys, values, out, *scratch):
    held_lengths, held_offsets, held_queries, held_keys, held_values, small_sems, key_sem, value_sem = scratch
    small = [
        pltpu.make_async_copy(source, target, small_sems.at[i])
        for i, (source, target) in enumerate(
            ((queries, held_queries), (lengths, held_lengths), (offsets, held_offsets))
        )
    ]
    key_copy = pltpu.make_async_copy(keys, held_keys, key_sem)
    value_copy = pltpu.make_async_copy(values, held_values, value_sem)
    for copy in [key_copy, *small, value_copy]:
        copy.start()
    chip = (lax.axis_index("y") * FAR + lax.axis_index("far")) * NEAR + lax.axis_index("near")
    index = chip * CORES + lax.axis_index("core")
    positions = index * CTX_DEV + lax.broadcasted_iota(jnp.int32, (ROWS, CTX_DEV), 1)
    draft = lax.broadcasted_iota(jnp.int32, (ROWS, 1), 0) // HEADS
    head = lax.rem(lax.broadcasted_iota(jnp.int32, (ROWS, LANES), 0), HEADS)
    slot, is_top = stat_lanes(ROWS)
    for copy in small:
        copy.wait()
    key_copy.wait()
    weights = []
    for b in range(BATCH):
        scores = jnp.dot(held_queries[b, 0], held_keys[b, 0], preferred_element_type=jnp.float32)
        scores = scores * DH ** (-0.5)
        offset = jnp.full((ROWS, 1), held_offsets[b, 0], jnp.int32)
        for j in range(1, DRAFT):
            offset = jnp.where(draft == j, held_offsets[b, j], offset)
        seen = positions < held_lengths[b] - offset
        scores = jnp.where(seen, scores, masked_score)
        block_max = jnp.max(scores, axis=1, keepdims=True)
        weight = jnp.where(seen, jnp.exp(scores - block_max), 0.0)
        block_sum = jnp.sum(weight, axis=1, keepdims=True)
        weights.append(weight.astype(jnp.bfloat16))
        stats = jnp.where(is_top, block_max, block_sum)
        stats = jnp.where(head == slot, stats, 0.0).reshape(DRAFT, HEADS, LANES)
        stats = jnp.sum(stats, axis=1)
        for j in range(DRAFT):
            out[b * DRAFT + j, :, HEADS * LANES :] = stats[j : j + 1]
    value_copy.wait()
    for b in range(BATCH):
        block_out = lax.dot_general(
            weights[b],
            held_values[b, 0], (((1,), (1,)), ((), ())), preferred_element_type=jnp.float32
        )
        for j in range(DRAFT):
            for h in range(HEADS):
                row = block_out[j * HEADS + h : j * HEADS + h + 1]
                out[b * DRAFT + j, :, h * LANES : (h + 1) * LANES] = row


def merge_near(parts, out):
    top, total, summed = merge(parts)
    _, is_top = stat_lanes(1)
    stats = jnp.where(is_top, top, pltpu.roll(total, SLOT // 2, 1))
    for h, row in enumerate(summed + [stats]):
        for i in range(FAR):
            out[i, :, h * LANES : (h + 1) * LANES] = row


def merge_far(parts, out):
    _, total, summed = merge(parts)
    rows = [row / total[:, h * SLOT : h * SLOT + 1] for h, row in enumerate(summed)]
    out[...] = jnp.broadcast_to(jnp.concatenate(rows, axis=0)[None], out.shape)


def project(attended, out_proj, out):
    total = jnp.zeros((TOKENS, COLS), jnp.float32)
    for h in range(HEADS):
        rows = attended[pl.ds(h, TOKENS, stride=HEADS), :].astype(jnp.bfloat16)
        total += lax.dot_general(
            rows, out_proj[0, h], (((1,), (1,)), ((), ())), preferred_element_type=jnp.float32
        )
    packed = jnp.concatenate([total[: TOKENS // 2], total[TOKENS // 2 :]], axis=1)
    out[...] = jnp.broadcast_to(packed[None], out.shape)


def add_groups(terms, out):
    packed = jnp.sum(terms[...], axis=0)
    out[: BATCH // 2] = packed[:, :COLS].reshape(BATCH // 2, DRAFT, COLS)
    out[BATCH // 2 :] = packed[:, COLS:].reshape(BATCH // 2, DRAFT, COLS)


def shards(queries, keys, values, lengths, offsets, out_proj):
    def packed(*shape):
        return jax.ShapeDtypeStruct(shape, jnp.float32)

    block = pl.pallas_call(
        attend_block,
        out_shape=packed(TOKENS, 1, MESSAGE),
        in_specs=[hbm] * 5,
        out_specs=vmem,
        scratch_shapes=[
            pltpu.SMEM((BATCH,), jnp.int32),
            pltpu.SMEM((BATCH, DRAFT), jnp.int32),
            pltpu.VMEM((BATCH, 1, ROWS, DH), jnp.bfloat16),
            pltpu.VMEM((BATCH, 1, DH, CTX_DEV), jnp.bfloat16),
            pltpu.VMEM((BATCH, 1, DH, CTX_DEV), jnp.bfloat16),
            pltpu.SemaphoreType.DMA((3,)),
            pltpu.SemaphoreType.DMA,
            pltpu.SemaphoreType.DMA,
        ],
        compiler_params=attend_params,
        name="attend_block",
    )(*(in_hbm(x) for x in (lengths, offsets, queries.swapaxes(2, 3), keys, values)))
    parts = lax.all_to_all(block, near_axes, 0, 0, axis_index_groups=near_order, tiled=True)
    copies = pl.pallas_call(
        merge_near, out_shape=packed(FAR, 1, MESSAGE), in_specs=[vmem], out_specs=vmem,
        compiler_params=small_params, name="merge_near"
    )(parts)
    parts = lax.all_to_all(
        copies, ("far", "near"), 0, 0, axis_index_groups=far_order, tiled=True
    )
    copies = pl.pallas_call(
        merge_far, out_shape=packed(TOKENS, HEADS, LANES), in_specs=[vmem], out_specs=vmem,
        compiler_params=small_params, name="merge_far"
    )(parts)
    rows = lax.all_to_all(copies, near_axes, 0, 0, axis_index_groups=near_order, tiled=True)
    copies = pl.pallas_call(
        project,
        out_shape=packed(HEAD, TOKENS * COLS // LANES, LANES),
        in_specs=[vmem, vmem],
        out_specs=vmem,
        compiler_params=small_params,
        name="project",
    )(rows.reshape(TOKENS * HEADS, LANES), out_proj.swapaxes(2, 3))
    terms = lax.all_to_all(copies, "head", 0, 0, axis_index_groups=head_order, tiled=True)
    return pl.pallas_call(
        add_groups,
        out_shape=jax.ShapeDtypeStruct((BATCH, DRAFT, COLS), jnp.float32),
        in_specs=[vmem],
        out_specs=vmem,
        compiler_params=small_params,
        name="add_groups",
    )(terms)


def solution(mesh):
    fine = Mesh(
        mesh.devices.reshape(Y, FAR, NEAR, CORES, HEAD), ("y", "far", "near", "core", "head")
    )
    seq = ("y", "far", "near", "core")
    placed = (
        P(None, "head", None, None),
        P(None, "head", None, seq),
        P(None, "head", None, seq),
        P(),
        P(),
        P("head", None, None, seq),
    )
    return jax.shard_map(
        shards, mesh=fine, in_specs=placed, out_specs=P(None, None, seq), check_vma=False
    )
```
